32 devices in a mesh: dp: 32 (over z, y, x, core).
Axes of the slice: x: 2, y: 2, z: 4, core: 2. Of those that a mesh axis runs over, the one named last changes fastest.
Arguments:
- hidden: bfloat16 [64, 512, 2048], P('dp'), may hold values from -6 to 6
- lengths: int32 [64], P('dp'), may hold values from 1 to 512, 16384 in all
- order: int32 [64], P('dp'), may hold values from 0 to 63, each once
- candidates: int32 [64, 64], replicated, may hold values from 0 to 16383, as said below
- norm_gain: float32 [2048], replicated, may hold values from 0.25 to 1.75
- w_query: bfloat16 [2048, 1024], P('dp'), may hold values from -1 to 1
- w_key: bfloat16 [2048, 1024], P('dp'), may hold values from -1 to 1
- w_value: bfloat16 [2048, 1024], P('dp'), may hold values from -0.125 to 0.125
- w_out: bfloat16 [1024, 2048], P('dp'), may hold values from -0.75 to 0.75
- index_rows: bfloat16 [16384, 2048], P('dp'), may hold values from -0.125 to 0.125
Outputs:
- scores: float32 [64, 64], P('dp')
The draws below stay inside these ranges and needn't reach their ends.
Inputs may be any that keep to these rules, and one draw needn't show every extreme that they name: The candidates of many texts may all lie in the index rows of one device: in every draw at least half of the texts have all 64 of their candidates in the 512 index rows of one device, the same device for all of them.
All inputs are finite; a program needn't handle non-finite values. No bound on the sum of `lengths` on one device may be relied on, other than what follows from the above.
Results may differ from the reference program's by a relative error of at most 0.005.
Values may be sent and summed in bfloat16 or wider, within the bound.
A program may use at most 128 MiB of HBM per device.

```python
import math
import jax
import jax.numpy as jnp
import numpy as np
from jax import lax

D = 2048
HEADS = 16
HEAD = 64
LMAX = 512
CAND = 64
ROWS_DEV = 512
HW = 1024
TEXTS = 64
ROWS = 16384


def weight_pair(key):
    base = jax.random.fold_in(key, 31)
    width = HEADS * HEAD
    key_part = jax.random.normal(jax.random.fold_in(base, 1), (D, width), jnp.float32) / math.sqrt(D)
    noise = jax.random.normal(jax.random.fold_in(base, 2), (D, width), jnp.float32) / math.sqrt(D * HEAD)
    query_part = noise
    return (jnp.clip(query_part, -1.0, 1.0), jnp.clip(key_part, -1.0, 1.0))


def draw_w_query(key, part):
    return weight_pair(key)[0].astype(jnp.bfloat16)


def draw_w_key(key, part):
    return weight_pair(key)[1].astype(jnp.bfloat16)


def draw_candidates(key, part):
    base = jax.random.fold_in(key, 57)
    shards = ROWS // ROWS_DEV
    chosen = jax.random.randint(jax.random.fold_in(base, 1), (), 0, shards, dtype=jnp.int32)
    ranking = jax.random.permutation(jax.random.fold_in(base, 2), jnp.arange(TEXTS, dtype=jnp.int32))
    nearby = chosen * ROWS_DEV + jax.random.randint(jax.random.fold_in(base, 3), (TEXTS, CAND), 0, ROWS_DEV, dtype=jnp.int32)
    first = jax.random.randint(jax.random.fold_in(base, 4), (TEXTS, CAND), 0, ROWS, dtype=jnp.int32)
    second = jax.random.randint(jax.random.fold_in(base, 5), (TEXTS, CAND), 0, ROWS, dtype=jnp.int32)
    relabel = jax.random.permutation(jax.random.fold_in(base, 6), jnp.arange(ROWS, dtype=jnp.int32))
    spread_rows = relabel[jnp.minimum(first, second)]
    result = jnp.where((ranking < TEXTS // 2)[:, None], nearby, spread_rows)
    coldest = jnp.argmax(ranking).astype(jnp.int32)
    result = result.at[coldest, 0].set(0).at[coldest, 1].set(ROWS - 1)
    return result.astype(jnp.int32)


def levels(rng, extent, pieces, least, high):
    gain = 1.0
    for dim, blocks in pieces:
        heights = jax.random.uniform(jax.random.fold_in(jax.random.fold_in(rng, 6), dim), (blocks,), jnp.float32, least / len(pieces), high / len(pieces))
        gain = gain * jnp.repeat(jnp.exp(heights), extent[dim] // blocks).reshape((-1,) + (1,) * (len(extent) - 1 - dim))
    return gain


def split_up(count, total, most, slope):
    portions = [(1 << 20) // math.isqrt(standing ** slope) + 1 for standing in range(2, count + 1)]
    rest, holding = total - most - (count - 1), [1] * (count - 1)
    while rest > 0:
        free = [i for i in range(count - 1) if holding[i] < most]
        mass, left = sum([portions[i] for i in free]), rest
        for i in free:
            addition = min(most - holding[i], max(1, left * portions[i] // mass), rest)
            holding[i] = holding[i] + addition
            rest = rest - addition
    return np.array([most] + holding)


def ragged_sizes(own_key, count, total, bound, slope):
    if count == 2:
        one = jax.random.randint(own_key, (), max(1, total - bound), min(bound, total - 1) + 1)
        return jnp.stack([one, total - one])
    sizes = jnp.asarray(split_up(count, total, bound, slope), jnp.int32)
    pairs = (count - 1) // 2
    giver, receiver = sizes[1:1 + 2 * pairs:2], sizes[2:2 + 2 * pairs:2]
    slack = jnp.minimum(giver - 1, bound - receiver)
    moved = jax.random.randint(jax.random.fold_in(own_key, 1), (pairs,), 0, 1 << 20) % (slack + 1)
    sizes = sizes.at[1:1 + 2 * pairs:2].set(giver - moved).at[2:2 + 2 * pairs:2].set(receiver + moved)
    return sizes[jax.random.permutation(jax.random.fold_in(own_key, 2), count)]


def gaussian(own_key, extent, scale, bound, cuts=(), held_as=jnp.bfloat16):
    values = scale * jax.random.normal(own_key, extent, jnp.float32)
    if cuts:
        values = values * levels(own_key, extent, cuts, -0.22, 0.18)
    return jnp.clip(values, -bound, bound).astype(held_as)


def setup_inputs(seed: int = 0) -> dict:
    seeds = jax.random.split(jax.random.key(seed), 11)
    return {
        "hidden": gaussian(seeds[0], (TEXTS, LMAX, D), 1.0, 6.0, ((0, 32),)),
        "lengths": ragged_sizes(seeds[1], TEXTS, TEXTS * LMAX // 2, LMAX, 2).astype(jnp.int32),
        "order": jax.random.permutation(seeds[2], TEXTS).astype(jnp.int32),
        "candidates": draw_candidates(jax.random.fold_in(seeds[10], 71), 0),
        "norm_gain": jnp.clip(1.0 + 0.15 * jax.random.normal(seeds[4], (D,), jnp.float32), 0.25, 1.75),
        "w_query": draw_w_query(jax.random.fold_in(seeds[10], 71), 0),
        "w_key": draw_w_key(jax.random.fold_in(seeds[10], 71), 0),
        "w_value": gaussian(seeds[7], (D, HW), D ** -0.5, 0.125, ((0, 32),)),
        "w_out": gaussian(seeds[8], (HW, D), HEAD ** -0.5, 0.75, ((0, 32),)),
        "index_rows": gaussian(seeds[9], (ROWS, D), D ** -0.5, 0.125, ((0, 32),)),
    }


def encode_text(text, length, norm_gain, w_query, w_key, w_value, w_out):
    values_f = text.astype(jnp.float32)
    meansq = lax.optimization_barrier(jnp.mean(values_f * values_f, axis=-1, keepdims=True))
    normed = (values_f * lax.rsqrt(meansq + 1e-06) * norm_gain).astype(jnp.bfloat16)
    queries = jnp.dot(normed, w_query, preferred_element_type=jnp.float32).astype(jnp.bfloat16)
    key_side = jnp.dot(normed, w_key, preferred_element_type=jnp.float32).astype(jnp.bfloat16)
    value_side = jnp.dot(normed, w_value, preferred_element_type=jnp.float32).astype(jnp.bfloat16)
    queries = queries.reshape(LMAX, HEADS, HEAD).astype(jnp.float32)
    key_side = key_side.reshape(LMAX, HEADS, HEAD).astype(jnp.float32)
    value_side = value_side.reshape(LMAX, HEADS, HEAD).astype(jnp.float32)
    logits = jnp.einsum('qhd,khd->hqk', queries, key_side)
    valid = jnp.arange(LMAX, dtype=jnp.int32) < length
    logits = jnp.where(valid[None, None, :], logits, jnp.float32(-1e+30))
    probs = jax.nn.softmax(logits, axis=-1).astype(jnp.bfloat16)
    context = jnp.einsum('hqk,khd->qhd', probs.astype(jnp.float32), value_side)
    context = context.astype(jnp.bfloat16).reshape(LMAX, HEADS * HEAD)
    layer_out = values_f + jnp.dot(context, w_out, preferred_element_type=jnp.float32)
    pooled = lax.optimization_barrier(jnp.sum(jnp.where(valid[:, None], layer_out, jnp.float32(0.0)), axis=0)) / length.astype(jnp.float32)
    unit = pooled * lax.rsqrt(jnp.mean(pooled * pooled) + 1e-06)
    return unit.astype(jnp.bfloat16)

def reference(hidden, lengths, order, candidates, norm_gain, w_query, w_key, w_value, w_out, index_rows):

    def one_text(pair):
        return encode_text(pair[0], pair[1], norm_gain, w_query, w_key, w_value, w_out)
    units = lax.map(one_text, (hidden, lengths))
    cand_proc = candidates[order]

    def score_text(pair):
        rows = index_rows[pair[1]].astype(jnp.float32)
        return jnp.dot(rows, pair[0].astype(jnp.float32), precision=lax.Precision.HIGHEST)
    scores_proc = lax.map(score_text, (units, cand_proc))
    scores = jnp.zeros((TEXTS, CAND), jnp.float32).at[order].set(scores_proc)
    return scores
```

```python
import functools

import jax
import jax.numpy as jnp
from jax import lax
from jax.experimental import pallas as pl
from jax.experimental.pallas import tpu as pltpu
from jax.sharding import PartitionSpec as P

HEAD = 64
MESH = pl.DeviceIdType.MESH
F32 = jnp.float32
BF16 = jnp.bfloat16


def grid_of(count):
    chips = count // 2
    side = 4 if chips >= 64 else 2
    return chips // (side * side), side, side


def split_rows(value):
    high = value.astype(BF16)
    low = (value - high.astype(F32)).astype(BF16)
    return jnp.concatenate([high, low], axis=0)


def encode_kernel(
    count, gather_out, lengths_ref, hidden_hbm, gain_ref, wq_hbm, wk_hbm, wv_hbm, wo_hbm,
    unit_ref, hidden_ref, normed_ref, gq, gk, gv, go, q_ref, k_ref, psum_ref, send, recv, local,
):
    planes, rows, cols = grid_of(count)
    me = lax.axis_index("dp")
    core = lax.rem(me, 2)
    b = lax.rem(me // 2, cols)
    a = lax.rem(me // (2 * cols), rows)
    z = me // (2 * cols * rows)
    texts = lengths_ref.shape[0]
    slots, width = hidden_ref.shape
    lmax = slots // texts
    heads = q_ref.shape[1] // HEAD

    def device(zz, aa, bb, cc):
        return ((zz * rows + aa) * cols + bb) * 2 + cc

    def others(size, own):
        return [lax.rem(own + step, size) for step in range(1, size)]

    z_line = [device(o, a, b, core) for o in others(planes, z)]
    a_line = [device(z, o, b, core) for o in others(rows, a)]
    b_line = [device(z, a, o, core) for o in others(cols, b)]
    twin = device(z, a, b, 1 - core)

    hidden_copy = pltpu.make_async_copy(hidden_hbm, hidden_ref, local.at[0])
    hidden_copy.start()

    pieces = []
    for source, held in ((wq_hbm, gq), (wk_hbm, gk)):
        half = source.shape[1] // 2
        pieces += [(source, held, 0, half), (source, held, half, half)]
    pieces = [pieces[0], pieces[2], pieces[1], pieces[3]]
    for source, held in ((wv_hbm, gv), (wo_hbm, go)):
        if source is wo_hbm and not gather_out:
            continue
        half = source.shape[1] // 2
        pieces += [(source, held, 0, half), (source, held, half, half)]

    local_copies = []
    for i, (source, held, start, size) in enumerate(pieces):
        copy = pltpu.make_async_copy(
            source.at[:, pl.ds(start, size)],
            held.at[z, a, b, core, :, pl.ds(start, size)],
            local.at[1 + i],
        )
        copy.start()
        local_copies.append(copy)
    if not gather_out:
        out_copy = pltpu.make_async_copy(wo_hbm, go, local.at[1 + len(pieces)])
        out_copy.start()

    barrier = pltpu.get_barrier_semaphore()
    partners = z_line + a_line + b_line + [twin]
    for other in partners:
        pl.semaphore_signal(barrier, inc=1, device_id=(other,), device_id_type=MESH)
    pl.semaphore_wait(barrier, len(partners))

    stages = []
    for i, (source, held, start, size) in enumerate(pieces):
        slot = 0
        half = size // 2
        first, second = pl.ds(start, half), pl.ds(start + half, half)
        whole = pl.ds(start, size)
        plan = ([], [], [], [])

        def add(stage, src, dst, target):
            nonlocal slot
            plan[stage].append(
                pltpu.make_async_remote_copy(
                    src_ref=src, dst_ref=dst, send_sem=send.at[i, slot],
                    recv_sem=recv.at[i, slot], device_id=(target,), device_id_type=MESH,
                )
            )
            slot += 1

        for target in z_line:
            add(0, source.at[:, whole], held.at[z, a, b, core, :, whole], target)
        for target in b_line:
            part = held.at[:, a, b, core, :, first]
            add(1, part, part, target)
        for target in a_line:
            part = held.at[:, a, b, core, :, second]
            add(1, part, part, target)
        for target in a_line:
            part = held.at[:, a, :, core, :, first]
            add(2, part, part, target)
        for target in b_line:
            part = held.at[:, :, b, core, :, second]
            add(2, part, part, target)
        part = held.at[:, :, :, core, :, whole]
        add(3, part, part, twin)
        stages.append(plan)

    def begin(piece, stage):
        if 0 <= piece < len(pieces):
            if stage == 1:
                local_copies[piece].wait()
            for copy in stages[piece][stage]:
                copy.start()

    def finish(piece, stage):
        if 0 <= piece < len(pieces):
            for copy in stages[piece][stage]:
                copy.wait()

    def advance(step):
        finish(step, 0)
        begin(step, 1)
        begin(step + 2, 0)
        finish(step - 1, 1)
        begin(step - 1, 2)
        finish(step - 2, 2)
        begin(step - 2, 3)
        finish(step - 3, 3)

    def norm_rows():
        tile = 128

        @pl.loop(0, slots // tile)
        def _(i):
            at = pl.ds(pl.multiple_of(i * tile, tile), tile)
            x = hidden_ref[at, :].astype(F32)
            mean = jnp.mean(x * x, axis=-1, keepdims=True)
            normed_ref[at, :] = (x * lax.rsqrt(mean + 1e-06) * gain_ref[...]).astype(BF16)

    def project(held, out, start, size):
        tile = 256

        @pl.loop(0, slots // tile)
        def _(i):
            at = pl.ds(pl.multiple_of(i * tile, tile), tile)
            for c in range(start, start + size, 256):
                w = held[:, :, :, :, :, c:c + 256].reshape(width, 256)
                out[at, c:c + 256] = jnp.dot(
                    normed_ref[at, :], w, preferred_element_type=F32
                ).astype(BF16)

    def attend(head_start, head_stop):
        lane = lax.broadcasted_iota(jnp.int32, (1, 2 * HEAD), 1)
        key_slot = lax.broadcasted_iota(jnp.int32, (1, lmax), 1)
        query_slot = lax.broadcasted_iota(jnp.int32, (lmax, 1), 0)
        for t in range(texts):
            length = lengths_ref[t]
            key_valid = key_slot < length
            query_valid = query_slot < length

            @pl.loop(head_start // 2, head_stop // 2)
            def _(pair):
                at = pl.ds(pl.multiple_of(pair * 2 * HEAD, 2 * HEAD), 2 * HEAD)
                q = q_ref[t * lmax:(t + 1) * lmax, at]
                k = k_ref[t * lmax:(t + 1) * lmax, at]
                sums = []
                for side in range(2):
                    q_one = jnp.where((lane // HEAD) == side, q, jnp.zeros_like(q))
                    logits = lax.dot_general(
                        q_one, k, (((1,), (1,)), ((), ())), preferred_element_type=F32
                    )
                    logits = jnp.where(key_valid, logits, F32(-1e30))
                    top = jnp.max(logits, axis=1, keepdims=True)
                    e = jnp.exp(logits - top)
                    weight = jnp.where(
                        query_valid, 1.0 / jnp.sum(e, axis=1, keepdims=True), F32(0.0)
                    )
                    sums.append(jnp.sum(e * weight, axis=0, keepdims=True))
                psum_ref[t, pl.ds(pair, 1), 0:lmax] = sums[0]
                psum_ref[t, pl.ds(pair, 1), lmax:2 * lmax] = sums[1]

    begin(0, 0)
    begin(1, 0)
    hidden_copy.wait()
    norm_rows()
    half_width = q_ref.shape[1] // 2
    quarter = heads // 4
    combined = []

    def combine():
        for t in range(texts):
            both = jnp.concatenate(
                [psum_ref[t, :, 0:lmax], psum_ref[t, :, lmax:2 * lmax]], axis=0
            )
            part = jnp.dot(
                split_rows(both), normed_ref[t * lmax:(t + 1) * lmax, :],
                preferred_element_type=F32,
            )
            combined.append(part[0:heads] + part[heads:2 * heads])

    for step in range(len(pieces) + 3):
        advance(step)
        if step == 3:
            project(gq, q_ref, 0, half_width)
        elif step == 4:
            project(gk, k_ref, 0, half_width)
            attend(0, quarter)
        elif step == 5:
            project(gq, q_ref, half_width, half_width)
            attend(quarter, 2 * quarter)
        elif step == 6:
            project(gk, k_ref, half_width, half_width)
            attend(2 * quarter, 3 * quarter)
        elif step == 7:
            attend(3 * quarter, heads)
            combine()
    if not gather_out:
        out_copy.wait()

    stacked = split_rows(jnp.concatenate(combined, axis=0))
    features = gv.shape[-1]
    lane = lax.broadcasted_iota(jnp.int32, (heads, features), 1)
    row = lax.broadcasted_iota(jnp.int32, (heads, features), 0)
    head = jnp.where(row < heads // 2, 2 * row, 2 * (row - heads // 2) + 1)
    pieces_v = []
    for c in range(0, features, 256):
        w = gv[:, :, :, :, :, c:c + 256].reshape(width, 256)
        pieces_v.append(jnp.dot(stacked, w, preferred_element_type=F32))
    spread = jnp.concatenate(pieces_v, axis=1)
    spread = spread[0:texts * heads] + spread[texts * heads:2 * texts * heads]
    contexts = [
        jnp.sum(
            jnp.where(lane // HEAD == head, spread[t * heads:(t + 1) * heads], F32(0.0)),
            axis=0, keepdims=True,
        )
        for t in range(texts)
    ]
    key_slot = lax.broadcasted_iota(jnp.int32, (16, lmax), 1)
    for t in range(texts):
        context = jnp.broadcast_to(contexts[t], (8, features))
        both = split_rows(context)
        valid = jnp.where(key_slot < lengths_ref[t], 1.0, 0.0).astype(BF16)
        total = jnp.dot(
            valid, hidden_ref[t * lmax:(t + 1) * lmax, :], preferred_element_type=F32
        )[0:8]
        outs = []
        for c in range(0, width, 512):
            if gather_out:
                w = go[:, :, :, :, :, c:c + 512].reshape(features, 512)
            else:
                w = go[:, c:c + 512]
            piece = jnp.dot(both, w, preferred_element_type=F32)
            outs.append(piece[0:8] + piece[8:16])
        pooled = (total + jnp.concatenate(outs, axis=1)) / lengths_ref[t].astype(F32)
        mean = jnp.mean(pooled * pooled, axis=-1, keepdims=True)
        unit_ref[t:t + 1, :] = (pooled * lax.rsqrt(mean + 1e-06))[0:1]


def encode(count, lengths, hidden, gain, w_query, w_key, w_value, w_out):
    planes, rows, cols = grid_of(count)
    texts, lmax, width = hidden.shape
    slots, features = texts * lmax, w_query.shape[1]
    gather_out = w_out.shape[0] % 16 == 0
    if not gather_out:
        w_out = lax.all_gather(w_out, "dp", axis=0, tiled=True)
    lead = (planes, rows, cols, 2)
    held = pltpu.VMEM(lead + w_query.shape, BF16)
    copies = planes - 1 + 2 * (rows - 1 + cols - 1) + 1
    return pl.pallas_call(
        functools.partial(encode_kernel, count, gather_out),
        out_shape=jax.ShapeDtypeStruct((texts, width), F32),
        in_specs=[
            pl.BlockSpec(memory_space=pltpu.SMEM),
            pl.BlockSpec(memory_space=pl.ANY),
            pl.BlockSpec(memory_space=pltpu.VMEM),
            pl.BlockSpec(memory_space=pl.ANY),
            pl.BlockSpec(memory_space=pl.ANY),
            pl.BlockSpec(memory_space=pl.ANY),
            pl.BlockSpec(memory_space=pl.ANY),
        ],
        out_specs=pl.BlockSpec(memory_space=pltpu.VMEM),
        scratch_shapes=[
            pltpu.VMEM((slots, width), BF16),
            pltpu.VMEM((slots, width), BF16),
            held, held, held,
            pltpu.VMEM((lead if gather_out else ()) + w_out.shape, BF16),
            pltpu.VMEM((slots, features), BF16),
            pltpu.VMEM((slots, features), BF16),
            pltpu.VMEM((texts, features // HEAD // 2, 2 * lmax), F32),
            pltpu.SemaphoreType.DMA((8, copies)),
            pltpu.SemaphoreType.DMA((8, copies)),
            pltpu.SemaphoreType.DMA((10,)),
        ],
        compiler_params=pltpu.CompilerParams(
            collective_id=0, has_side_effects=True, vmem_limit_bytes=56 * 1024 * 1024
        ),
        cost_estimate=pl.CostEstimate(
            flops=10 ** 10, bytes_accessed=24 * 2 ** 20, transcendentals=2 ** 23
        ),
    )(lengths, hidden.reshape(slots, width), gain.reshape(1, width), w_query, w_key, w_value, w_out)


def score_kernel(
    count, note_ref, index_ref, cand_ref, out_ref, got, mine, back, send, recv, send2, recv2
):
    me = lax.axis_index("dp")
    texts = out_ref.shape[0]
    total = count * texts
    rows_dev, width = index_ref.shape
    wide = width // 8

    def to(step):
        return lax.rem(me + step, count)

    def source(step):
        return lax.rem(me + count - step, count)

    barrier = pltpu.get_barrier_semaphore()

    @pl.loop(1, count)
    def _(step):
        pl.semaphore_signal(barrier, inc=1, device_id=(to(step),), device_id_type=MESH)

    pl.semaphore_wait(barrier, count - 1)

    def note_copy(step, place, target):
        return pltpu.make_async_remote_copy(
            src_ref=note_ref, dst_ref=got.at[place], send_sem=send.at[step],
            recv_sem=recv.at[step], device_id=(target,), device_id_type=MESH,
        )

    @pl.loop(1, count)
    def _(step):
        note_copy(step, me, to(step)).start()

    got[me] = note_ref[...]

    @pl.loop(1, count)
    def _(step):
        note_copy(step, source(step), to(step)).wait_recv()

    flat = got[...].reshape(count * texts * 8, wide + 128)
    data = flat[:, 0:wide]
    numbers = flat[:, wide:wide + 128].astype(F32).T[0:1, :].astype(jnp.int32)
    span = count * texts * 8
    lane = lax.broadcasted_iota(jnp.int32, (total, span), 1)
    row = lax.broadcasted_iota(jnp.int32, (total, span), 0)
    same = numbers == row
    scores = jnp.zeros((total, rows_dev), F32)
    for k in range(8):
        pick = jnp.where(same & (lax.rem(lane, 8) == k), 1.0, 0.0).astype(BF16)
        unit = jnp.dot(pick, data, preferred_element_type=F32).astype(BF16)
        scores += lax.dot_general(
            unit, index_ref[:, k * wide:(k + 1) * wide], (((1,), (1,)), ((), ())),
            preferred_element_type=F32,
        )
    within = cand_ref[...] - me * rows_dev
    slot = lax.broadcasted_iota(jnp.int32, (1, 1, rows_dev), 2)
    for r in range(0, total, 8):
        hit = within[r:r + 8][:, :, None] == slot
        part = jnp.sum(jnp.where(hit, scores[r:r + 8][:, None, :], F32(0.0)), axis=2)
        for j in range(0, 8, texts):
            mine[(r + j) // texts] = part[j:j + texts, :]

    def back_copy(step, target, place):
        return pltpu.make_async_remote_copy(
            src_ref=mine.at[target], dst_ref=back.at[place], send_sem=send2.at[step],
            recv_sem=recv2.at[step], device_id=(target,), device_id_type=MESH,
        )

    @pl.loop(1, count)
    def _(step):
        back_copy(step, to(step), me).start()

    back[me] = mine[me]

    @pl.loop(1, count)
    def _(step):
        back_copy(step, to(step), source(step)).wait_recv()

    out_ref[...] = jnp.sum(back[...], axis=0)

    @pl.loop(1, count)
    def _(step):
        note_copy(step, source(step), to(step)).wait_send()
        back_copy(step, to(step), source(step)).wait_send()


def score(count, note, index_rows, candidates, texts):
    cand = candidates.shape[1]
    return pl.pallas_call(
        functools.partial(score_kernel, count),
        out_shape=jax.ShapeDtypeStruct((texts, cand), F32),
        in_specs=[pl.BlockSpec(memory_space=pltpu.VMEM)] * 3,
        out_specs=pl.BlockSpec(memory_space=pltpu.VMEM),
        scratch_shapes=[
            pltpu.VMEM((count,) + note.shape, BF16),
            pltpu.VMEM((count, texts, cand), F32),
            pltpu.VMEM((count, texts, cand), F32),
            pltpu.SemaphoreType.DMA((count,)),
            pltpu.SemaphoreType.DMA((count,)),
            pltpu.SemaphoreType.DMA((count,)),
            pltpu.SemaphoreType.DMA((count,)),
        ],
        compiler_params=pltpu.CompilerParams(
            collective_id=1, has_side_effects=True, vmem_limit_bytes=48 * 1024 * 1024
        ),
        cost_estimate=pl.CostEstimate(
            flops=3 * 10 ** 8, bytes_accessed=4 * 2 ** 20, transcendentals=0
        ),
    )(note, index_rows, candidates)


def solution(mesh):
    count = mesh.shape["dp"]

    def per_device(
        hidden, lengths, order, candidates, norm_gain, w_query, w_key, w_value, w_out, index_rows
    ):
        texts, _, width = hidden.shape
        unit = encode(count, lengths, hidden, norm_gain, w_query, w_key, w_value, w_out)
        wide = width // 8
        number = jnp.broadcast_to(order.astype(BF16)[:, None, None], (texts, 8, 128))
        note = jnp.concatenate([unit.reshape(texts, 8, wide).astype(BF16), number], axis=2)
        note = note.reshape(texts * 8, wide + 128)
        return score(count, note, index_rows, candidates, texts)

    return jax.shard_map(
        per_device,
        mesh=mesh,
        in_specs=(
            P("dp", None, None),
            P("dp"),
            P("dp"),
            P(),
            P(),
            P("dp", None),
            P("dp", None),
            P("dp", None),
            P("dp", None),
            P("dp", None),
        ),
        out_specs=P("dp", None),
        check_vma=False,
    )
```

```python
import functools

import jax
import jax.numpy as jnp
from jax import lax
from jax.experimental import pallas as pl
from jax.experimental.pallas import tpu as pltpu
from jax.sharding import PartitionSpec as P

HEAD = 64
MESH = pl.DeviceIdType.MESH
F32 = jnp.float32
BF16 = jnp.bfloat16


def grid_of(count):
    chips = count // 2
    side = 4 if chips >= 64 else 2
    return chips // (side * side), side, side


def split_rows(value):
    high = value.astype(BF16)
    low = (value - high.astype(F32)).astype(BF16)
    return jnp.concatenate([high, low], axis=0)


def kernel(
    count, lengths_ref, order_ref, hidden_hbm, gain_ref, wq_hbm, wk_hbm, wv_hbm, wo_hbm,
    index_hbm, cand_ref, out_ref,
    hidden_ref, normed_ref, gq, gk, gv, go, q_ref, k_ref, psum_ref, index_ref,
    context_mine, context_got, context_flat, part_mine, part_got,
    rows_ref, note_ref, got, mine, back,
    send, recv, local, send_o, recv_o, send_c, recv_c, send_p, recv_p,
    send_n, recv_n, send_s, recv_s,
):
    planes, rows, cols = grid_of(count)
    plane = rows * cols * 2
    me = lax.axis_index("dp")
    core = lax.rem(me, 2)
    b = lax.rem(me // 2, cols)
    a = lax.rem(me // (2 * cols), rows)
    z = me // plane
    place = lax.rem(me, plane)
    texts = lengths_ref.shape[0]
    slots, width = hidden_ref.shape
    lmax = slots // texts
    features = q_ref.shape[1]
    heads = features // HEAD
    span = 256

    def device(zz, aa, bb, cc):
        return ((zz * rows + aa) * cols + bb) * 2 + cc

    def others(size, own):
        return [lax.rem(own + step, size) for step in range(1, size)]

    z_line = [device(o, a, b, core) for o in others(planes, z)]
    a_line = [device(z, o, b, core) for o in others(rows, a)]
    b_line = [device(z, a, o, core) for o in others(cols, b)]
    twin = device(z, a, b, 1 - core)

    hidden_copy = pltpu.make_async_copy(hidden_hbm, hidden_ref, local.at[0])
    hidden_copy.start()

    pieces = []
    for start in range(0, features, span):
        pieces += [(wq_hbm, gq, start), (wk_hbm, gk, start)]
    for start in range(0, features, span):
        pieces += [(wv_hbm, gv, start)]
    blocks = features // span

    local_copies = []
    for i, (source, held, start) in enumerate(pieces):
        copy = pltpu.make_async_copy(
            source.at[:, pl.ds(start, span)],
            held.at[z, a, b, core, :, pl.ds(start, span)],
            local.at[3 + i],
        )
        copy.start()
        local_copies.append(copy)

    barrier = pltpu.get_barrier_semaphore()

    @pl.loop(1, count)
    def _(step):
        pl.semaphore_signal(
            barrier, inc=1, device_id=(lax.rem(me + step, count),), device_id_type=MESH
        )

    pl.semaphore_wait(barrier, count - 1)

    def remote(src, dst, send_sem, recv_sem, target):
        return pltpu.make_async_remote_copy(
            src_ref=src, dst_ref=dst, send_sem=send_sem, recv_sem=recv_sem,
            device_id=(target,), device_id_type=MESH,
        )

    stages = []
    for i, (source, held, start) in enumerate(pieces):
        half = span // 2
        first, second = pl.ds(start, half), pl.ds(start + half, half)
        whole = pl.ds(start, span)
        ends = []
        ends += [(0, source.at[:, whole], held.at[z, a, b, core, :, whole], t) for t in z_line]
        part = held.at[:, a, b, core, :, first]
        ends += [(1, part, part, t) for t in b_line]
        part = held.at[:, a, b, core, :, second]
        ends += [(1, part, part, t) for t in a_line]
        part = held.at[:, a, :, core, :, first]
        ends += [(2, part, part, t) for t in a_line]
        part = held.at[:, :, b, core, :, second]
        ends += [(2, part, part, t) for t in b_line]
        part = held.at[:, :, :, core, :, whole]
        ends += [(3, part, part, twin)]
        plan = ([], [], [], [])
        for slot, (stage, src, dst, target) in enumerate(ends):
            plan[stage].append(remote(src, dst, send.at[i, slot], recv.at[i, slot], target))
        stages.append(plan)

    def begin(piece, stage):
        if 0 <= piece < len(pieces):
            if stage == 1:
                local_copies[piece].wait()
            for copy in stages[piece][stage]:
                copy.start()

    def finish(piece, stage):
        if 0 <= piece < len(pieces):
            for copy in stages[piece][stage]:
                copy.wait()

    def advance(step):
        finish(step, 0)
        begin(step, 1)
        begin(step + 3, 0)
        finish(step - 1, 1)
        begin(step - 1, 2)
        finish(step - 2, 2)
        begin(step - 2, 3)
        finish(step - 3, 3)

    def norm_rows():
        tile = 128

        @pl.loop(0, slots // tile)
        def _(i):
            at = pl.ds(pl.multiple_of(i * tile, tile), tile)
            x = hidden_ref[at, :].astype(F32)
            mean = jnp.mean(x * x, axis=-1, keepdims=True)
            normed_ref[at, :] = (x * lax.rsqrt(mean + 1e-06) * gain_ref[...]).astype(BF16)

    def project(held, out, c):
        tile = 512

        @pl.loop(0, slots // tile)
        def _(i):
            at = pl.ds(pl.multiple_of(i * tile, tile), tile)
            w = held[:, :, :, :, :, c:c + span].reshape(width, span)
            out[at, c:c + span] = jnp.dot(
                normed_ref[at, :], w, preferred_element_type=F32
            ).astype(BF16)

    def attend(pair):
        lane = lax.broadcasted_iota(jnp.int32, (1, 2 * HEAD), 1)
        key_slot = lax.broadcasted_iota(jnp.int32, (1, lmax), 1)
        query_slot = lax.broadcasted_iota(jnp.int32, (lmax, 1), 0)
        at = pl.ds(pair * 2 * HEAD, 2 * HEAD)

        @pl.loop(0, texts)
        def _(t):
            length = lengths_ref[t]
            key_valid = key_slot < length
            query_valid = query_slot < length
            mine_rows = pl.ds(pl.multiple_of(t * lmax, lmax), lmax)
            q = q_ref[mine_rows, at]
            k = k_ref[mine_rows, at]
            for side in range(2):
                q_one = jnp.where((lane // HEAD) == side, q, jnp.zeros_like(q))
                logits = lax.dot_general(
                    q_one, k, (((1,), (1,)), ((), ())), preferred_element_type=F32
                )
                logits = jnp.where(key_valid, logits, F32(-1e30))
                top = jnp.max(logits, axis=1, keepdims=True)
                e = jnp.exp(logits - top)
                weight = jnp.where(
                    query_valid, 1.0 / jnp.sum(e, axis=1, keepdims=True), F32(0.0)
                )
                psum_ref[t, pair:pair + 1, side * lmax:(side + 1) * lmax] = jnp.sum(
                    e * weight, axis=0, keepdims=True
                )

    def combine():
        combined = []
        for t in range(texts):
            both = jnp.concatenate(
                [psum_ref[t, :, 0:lmax], psum_ref[t, :, lmax:2 * lmax]], axis=0
            )
            part = jnp.dot(
                split_rows(both), normed_ref[t * lmax:(t + 1) * lmax, :],
                preferred_element_type=F32,
            )
            combined.append(part[0:heads] + part[heads:2 * heads])
        return split_rows(jnp.concatenate(combined, axis=0))

    def value_piece(stacked, c):
        lane = c + lax.broadcasted_iota(jnp.int32, (heads, span), 1)
        row = lax.broadcasted_iota(jnp.int32, (heads, span), 0)
        head = jnp.where(row < heads // 2, 2 * row, 2 * (row - heads // 2) + 1)
        w = gv[:, :, :, :, :, c:c + span].reshape(width, span)
        spread = jnp.dot(stacked, w, preferred_element_type=F32)
        spread = spread[0:texts * heads] + spread[texts * heads:2 * texts * heads]
        for t in range(texts):
            context_mine[t:t + 1, c:c + span] = jnp.sum(
                jnp.where(lane // HEAD == head, spread[t * heads:(t + 1) * heads], F32(0.0)),
                axis=0, keepdims=True,
            )

    for piece in range(3):
        begin(piece, 0)
    out_local = pltpu.make_async_copy(wo_hbm, go.at[z], local.at[1])
    out_local.start()
    index_copy = pltpu.make_async_copy(index_hbm, index_ref, local.at[2])
    index_copy.start()
    out_copies = [
        remote(wo_hbm, go.at[z], send_o.at[i], recv_o.at[i], target)
        for i, target in enumerate(z_line)
    ]
    hidden_copy.wait()
    norm_rows()

    pairs = heads // 2
    done = 0
    stacked = None
    for step in range(len(pieces) + 3):
        advance(step)
        ready = step - 3
        if ready == 0:
            for copy in out_copies:
                copy.start()
        if 0 <= ready < 2 * blocks:
            if ready % 2 == 0:
                project(gq, q_ref, (ready // 2) * span)
            else:
                project(gk, k_ref, (ready // 2) * span)
        if 1 <= ready < 2 * blocks:
            attend(done)
            done += 1
        if ready == 2 * blocks:
            while done < pairs:
                attend(done)
                done += 1
            stacked = combine()
        if ready >= 2 * blocks:
            value_piece(stacked, (ready - 2 * blocks) * span)

    def plane_device(step):
        return z * plane + lax.rem(place + step, plane)

    def plane_source(step):
        return lax.rem(place + plane - step, plane)

    def context_copy(step):
        return remote(
            context_mine, context_got.at[place], send_c.at[step], recv_c.at[step],
            plane_device(step),
        )

    for step in range(1, plane):
        context_copy(step).start()
    context_got[place] = context_mine[...]
    out_local.wait()
    for copy in out_copies:
        copy.wait()
    rows_out = go.shape[1]
    depth = planes * rows_out
    feature = lax.broadcasted_iota(jnp.int32, (features, depth), 0)
    slot = lax.broadcasted_iota(jnp.int32, (features, depth), 1)
    wanted = (slot // rows_out) * (plane * rows_out) + place * rows_out + lax.rem(slot, rows_out)
    choose = jnp.where(feature == wanted, 1.0, 0.0).astype(BF16)
    key_slot = lax.broadcasted_iota(jnp.int32, (16, lmax), 1)
    totals = []
    for t in range(texts):
        valid = jnp.where(key_slot < lengths_ref[t], 1.0, 0.0).astype(BF16)
        totals.append(
            jnp.dot(
                valid, hidden_ref[t * lmax:(t + 1) * lmax, :], preferred_element_type=F32
            )[0:1]
        )
    for step in range(1, plane):
        remote(
            context_mine, context_got.at[plane_source(step)], send_c.at[step],
            recv_c.at[step], plane_device(step),
        ).wait()
    for j in range(plane):
        context_flat[j * texts:(j + 1) * texts, :] = context_got[j]
    group = plane * texts
    chosen = jnp.dot(split_rows(context_flat[...]), choose, preferred_element_type=F32)
    held_out = go[...].reshape(depth, width).astype(BF16)
    part = jnp.dot(chosen.astype(BF16), held_out, preferred_element_type=F32)
    part = part[0:group] + part[group:2 * group]
    for j in range(plane):
        part_mine[j] = part[j * texts:(j + 1) * texts, :]

    def part_copy(step, where):
        return remote(
            part_mine.at[lax.rem(place + step, plane)], part_got.at[where], send_p.at[step],
            recv_p.at[step], plane_device(step),
        )

    for step in range(1, plane):
        part_copy(step, place).start()
    part_got[place] = part_mine[place]
    for step in range(1, plane):
        part_copy(step, plane_source(step)).wait()
    summed = part_got[0]
    for j in range(1, plane):
        summed += part_got[j]
    wide = width // 8
    for t in range(texts):
        pooled = (totals[t] + summed[t:t + 1]) / lengths_ref[t].astype(F32)
        mean = jnp.mean(pooled * pooled, axis=-1, keepdims=True)
        unit = pooled * lax.rsqrt(mean + 1e-06)
        for k in range(8):
            rows_ref[t * 8 + k:t * 8 + k + 1, 0:wide] = unit[:, k * wide:(k + 1) * wide]
        rows_ref[t * 8:(t + 1) * 8, wide:wide + 128] = jnp.full(
            (8, 128), order_ref[t], jnp.int32
        ).astype(F32)
    note_ref[...] = rows_ref[...].astype(BF16)

    line = [
        remote(note_ref, got.at[z, place], send_n.at[i], recv_n.at[i], target)
        for i, target in enumerate(z_line)
    ]
    for copy in line:
        copy.start()
    got[z, place] = note_ref[...]
    for copy in line:
        copy.wait()

    def note_copy(step, where):
        return remote(
            got.at[:, where], got.at[:, where], send_n.at[planes - 1 + step],
            recv_n.at[planes - 1 + step], plane_device(step),
        )

    for step in range(1, plane):
        note_copy(step, place).start()
    index_copy.wait()
    for step in range(1, plane):
        note_copy(step, place).wait_send()
        note_copy(step, plane_source(step)).wait_recv()

    total = count * texts
    rows_dev = index_ref.shape[0]
    long = count * texts * 8
    flat = got[...].reshape(long, wide + 128)
    data = flat[:, 0:wide]
    numbers = flat[:, wide:wide + 128].astype(F32).T[0:1, :].astype(jnp.int32)
    lane = lax.broadcasted_iota(jnp.int32, (total, long), 1)
    row = lax.broadcasted_iota(jnp.int32, (total, long), 0)
    same = numbers == row
    scores = jnp.zeros((total, rows_dev), F32)
    for k in range(8):
        pick = jnp.where(same & (lax.rem(lane, 8) == k), 1.0, 0.0).astype(BF16)
        unit = jnp.dot(pick, data, preferred_element_type=F32).astype(BF16)
        scores += lax.dot_general(
            unit, index_ref[:, k * wide:(k + 1) * wide], (((1,), (1,)), ((), ())),
            preferred_element_type=F32,
        )
    within = cand_ref[...] - me * rows_dev
    slot = lax.broadcasted_iota(jnp.int32, (1, 1, rows_dev), 2)
    for r in range(0, total, 8):
        hit = within[r:r + 8][:, :, None] == slot
        found = jnp.sum(jnp.where(hit, scores[r:r + 8][:, None, :], F32(0.0)), axis=2)
        for j in range(0, 8, texts):
            mine[(r + j) // texts] = found[j:j + texts, :]

    def back_copy(step, where):
        target = lax.rem(me + step, count)
        return remote(
            mine.at[target], back.at[where], send_s.at[step], recv_s.at[step], target
        )

    @pl.loop(1, count)
    def _(step):
        back_copy(step, me).start()

    back[me] = mine[me]

    @pl.loop(1, count)
    def _(step):
        back_copy(step, lax.rem(me + count - step, count)).wait()

    out_ref[...] = jnp.sum(back[...], axis=0)


def solution(mesh):
    count = mesh.shape["dp"]
    planes, rows, cols = grid_of(count)
    plane = rows * cols * 2

    def per_device(
        hidden, lengths, order, candidates, norm_gain, w_query, w_key, w_value, w_out, index_rows
    ):
        texts, lmax, width = hidden.shape
        slots, features = texts * lmax, w_query.shape[1]
        if w_out.shape[0] % 16:
            w_out = w_out.astype(F32)
        cand = candidates.shape[1]
        lead = (planes, rows, cols, 2)
        held = pltpu.VMEM(lead + w_query.shape, BF16)
        copies = planes - 1 + 2 * (rows - 1 + cols - 1) + 1
        pieces = 3 * features // 256
        note = (texts * 8, width // 8 + 128)
        dma = pltpu.SemaphoreType.DMA
        anywhere = pl.BlockSpec(memory_space=pl.ANY)
        scalar = pl.BlockSpec(memory_space=pltpu.SMEM)
        vector = pl.BlockSpec(memory_space=pltpu.VMEM)
        return pl.pallas_call(
            functools.partial(kernel, count),
            out_shape=jax.ShapeDtypeStruct((texts, cand), F32),
            in_specs=[scalar, scalar, anywhere, vector] + [anywhere] * 5 + [vector],
            out_specs=vector,
            scratch_shapes=[
                pltpu.VMEM((slots, width), BF16),
                pltpu.VMEM((slots, width), BF16),
                held, held, held,
                pltpu.VMEM((planes,) + w_out.shape, w_out.dtype),
                pltpu.VMEM((slots, features), BF16),
                pltpu.VMEM((slots, features), BF16),
                pltpu.VMEM((texts, features // HEAD // 2, 2 * lmax), F32),
                pltpu.VMEM(index_rows.shape, BF16),
                pltpu.VMEM((texts, features), F32),
                pltpu.VMEM((plane, texts, features), F32),
                pltpu.VMEM((plane * texts, features), F32),
                pltpu.VMEM((plane, texts, width), F32),
                pltpu.VMEM((plane, texts, width), F32),
                pltpu.VMEM(note, F32),
                pltpu.VMEM(note, BF16),
                pltpu.VMEM((planes, plane) + note, BF16),
                pltpu.VMEM((count, texts, cand), F32),
                pltpu.VMEM((count, texts, cand), F32),
                dma((pieces, copies)), dma((pieces, copies)), dma((pieces + 3,)),
                dma((planes,)), dma((planes,)), dma((plane,)), dma((plane,)),
                dma((plane,)), dma((plane,)), dma((planes + plane,)), dma((planes + plane,)),
                dma((count,)), dma((count,)),
            ],
            compiler_params=pltpu.CompilerParams(
                collective_id=0, has_side_effects=True, vmem_limit_bytes=56 * 1024 * 1024
            ),
            cost_estimate=pl.CostEstimate(
                flops=10 ** 10, bytes_accessed=24 * 2 ** 20, transcendentals=2 ** 23
            ),
        )(
            lengths, order, hidden.reshape(slots, width), norm_gain.reshape(1, width),
            w_query, w_key, w_value, w_out, index_rows, candidates,
        )

    return jax.shard_map(
        per_device,
        mesh=mesh,
        in_specs=(
            P("dp", None, None),
            P("dp"),
            P("dp"),
            P(),
            P(),
            P("dp", None),
            P("dp", None),
            P("dp", None),
            P("dp", None),
            P("dp", None),
        ),
        out_specs=P("dp", None),
        check_vma=False,
    )
```

```python
import functools

import jax
import jax.numpy as jnp
from jax import lax
from jax.experimental import pallas as pl
from jax.experimental.pallas import tpu as pltpu
from jax.sharding import PartitionSpec as P

HEAD = 64
MESH = pl.DeviceIdType.MESH
F32 = jnp.float32
BF16 = jnp.bfloat16


def grid_of(count):
    chips = count // 2
    side = 4 if chips >= 64 else 2
    return chips // (side * side), side, side


def split_rows(value):
    high = value.astype(BF16)
    low = (value - high.astype(F32)).astype(BF16)
    return jnp.concatenate([high, low], axis=0)


def kernel(
    count, lengths_ref, order_ref, hidden_hbm, gain_ref, wq_hbm, wk_hbm, wv_hbm, wo_hbm,
    index_hbm, cand_ref, out_ref,
    hidden_ref, normed_ref, gq, gk, gv, go, q_ref, k_ref, psum_ref, index_ref,
    context_mine, context_got, context_flat, part_mine, part_got,
    rows_ref, note_ref, got, mine, back,
    send, recv, local, send_o, recv_o, send_c, recv_c, send_p, recv_p,
    send_n, recv_n, send_s, recv_s,
):
    planes, rows, cols = grid_of(count)
    plane = rows * cols * 2
    me = lax.axis_index("dp")
    core = lax.rem(me, 2)
    b = lax.rem(me // 2, cols)
    a = lax.rem(me // (2 * cols), rows)
    z = me // plane
    place = lax.rem(me, plane)
    texts = lengths_ref.shape[0]
    slots, width = hidden_ref.shape
    lmax = slots // texts
    features = q_ref.shape[1]
    heads = features // HEAD
    span = 256

    def device(zz, aa, bb, cc):
        return ((zz * rows + aa) * cols + bb) * 2 + cc

    def others(size, own):
        return [lax.rem(own + step, size) for step in range(1, size)]

    z_line = [device(o, a, b, core) for o in others(planes, z)]
    a_line = [device(z, o, b, core) for o in others(rows, a)]
    b_line = [device(z, a, o, core) for o in others(cols, b)]
    twin = device(z, a, b, 1 - core)

    hidden_copy = pltpu.make_async_copy(hidden_hbm, hidden_ref, local.at[0])
    hidden_copy.start()

    pieces = []
    for start in range(0, features, span):
        pieces += [(wq_hbm, gq, start), (wk_hbm, gk, start)]
    for start in range(0, features, span):
        pieces += [(wv_hbm, gv, start)]
    blocks = features // span

    local_copies = []
    for i, (source, held, start) in enumerate(pieces):
        copy = pltpu.make_async_copy(
            source.at[:, pl.ds(start, span)],
            held.at[z, a, b, core, :, pl.ds(start, span)],
            local.at[3 + i],
        )
        copy.start()
        local_copies.append(copy)

    barrier = pltpu.get_barrier_semaphore()

    @pl.loop(1, count)
    def _(step):
        pl.semaphore_signal(
            barrier, inc=1, device_id=(lax.rem(me + step, count),), device_id_type=MESH
        )

    pl.semaphore_wait(barrier, count - 1)

    def remote(src, dst, send_sem, recv_sem, target):
        return pltpu.make_async_remote_copy(
            src_ref=src, dst_ref=dst, send_sem=send_sem, recv_sem=recv_sem,
            device_id=(target,), device_id_type=MESH,
        )

    stages = []
    for i, (source, held, start) in enumerate(pieces):
        half = span // 2
        first, second = pl.ds(start, half), pl.ds(start + half, half)
        whole = pl.ds(start, span)
        ends = []
        ends += [(0, source.at[:, whole], held.at[z, a, b, core, :, whole], t) for t in z_line]
        part = held.at[:, a, b, core, :, first]
        ends += [(1, part, part, t) for t in b_line]
        part = held.at[:, a, b, core, :, second]
        ends += [(1, part, part, t) for t in a_line]
        part = held.at[:, a, :, core, :, first]
        ends += [(2, part, part, t) for t in a_line]
        part = held.at[:, :, b, core, :, second]
        ends += [(2, part, part, t) for t in b_line]
        part = held.at[:, :, :, core, :, whole]
        ends += [(3, part, part, twin)]
        plan = ([], [], [], [])
        for slot, (stage, src, dst, target) in enumerate(ends):
            plan[stage].append(remote(src, dst, send.at[i, slot], recv.at[i, slot], target))
        stages.append(plan)

    def begin(piece, stage):
        if 0 <= piece < len(pieces):
            if stage == 1:
                local_copies[piece].wait()
            for copy in stages[piece][stage]:
                copy.start()

    def finish(piece, stage):
        if 0 <= piece < len(pieces):
            for copy in stages[piece][stage]:
                copy.wait()

    def advance(step):
        finish(step, 0)
        begin(step, 1)
        begin(step + 3, 0)
        finish(step - 1, 1)
        begin(step - 1, 2)
        finish(step - 2, 2)
        begin(step - 2, 3)
        finish(step - 3, 3)

    def norm_rows():
        tile = 128

        @pl.loop(0, slots // tile)
        def _(i):
            at = pl.ds(pl.multiple_of(i * tile, tile), tile)
            x = hidden_ref[at, :].astype(F32)
            mean = jnp.mean(x * x, axis=-1, keepdims=True)
            normed_ref[at, :] = (x * lax.rsqrt(mean + 1e-06) * gain_ref[...]).astype(BF16)

    def project(held, out, c):
        tile = 512

        @pl.loop(0, slots // tile)
        def _(i):
            at = pl.ds(pl.multiple_of(i * tile, tile), tile)
            w = held[:, :, :, :, :, c:c + span].reshape(width, span)
            out[at, c:c + span] = jnp.dot(
                normed_ref[at, :], w, preferred_element_type=F32
            ).astype(BF16)

    def attend(pair, t):
        lane = lax.broadcasted_iota(jnp.int32, (1, 2 * HEAD), 1)
        slot = lax.broadcasted_iota(jnp.int32, (lmax, 1), 0)
        valid = slot < lengths_ref[t]
        mask = jnp.where(valid, 0.0, -1e30).astype(BF16)
        at = pl.ds(pair * 2 * HEAD, 2 * HEAD)
        q = q_ref[t * lmax:(t + 1) * lmax, at]
        k = k_ref[t * lmax:(t + 1) * lmax, at]
        for side in range(2):
            spare = (1 - side) * HEAD
            unit = jnp.where(lane == spare, 1.0, 0.0).astype(BF16)
            q_one = jnp.where((lane // HEAD) == side, q, unit)
            k_one = jnp.where(lane == spare, mask, k)
            logits = lax.dot_general(
                q_one, k_one, (((1,), (1,)), ((), ())), preferred_element_type=F32
            )
            top = jnp.max(logits, axis=1, keepdims=True)
            e = jnp.exp(logits - top)
            weight = jnp.where(valid, 1.0 / jnp.sum(e, axis=1, keepdims=True), F32(0.0))
            psum_ref[t, pair:pair + 1, side * lmax:(side + 1) * lmax] = jnp.sum(
                e * weight, axis=0, keepdims=True
            )

    def combine():
        combined = []
        for t in range(texts):
            both = jnp.concatenate(
                [psum_ref[t, :, 0:lmax], psum_ref[t, :, lmax:2 * lmax]], axis=0
            )
            part = jnp.dot(
                split_rows(both), normed_ref[t * lmax:(t + 1) * lmax, :],
                preferred_element_type=F32,
            )
            combined.append(part[0:heads] + part[heads:2 * heads])
        return split_rows(jnp.concatenate(combined, axis=0))

    def value_piece(stacked, c):
        lane = c + lax.broadcasted_iota(jnp.int32, (heads, span), 1)
        row = lax.broadcasted_iota(jnp.int32, (heads, span), 0)
        head = jnp.where(row < heads // 2, 2 * row, 2 * (row - heads // 2) + 1)
        w = gv[:, :, :, :, :, c:c + span].reshape(width, span)
        spread = jnp.dot(stacked, w, preferred_element_type=F32)
        spread = spread[0:texts * heads] + spread[texts * heads:2 * texts * heads]
        for t in range(texts):
            context_mine[t:t + 1, c:c + span] = jnp.sum(
                jnp.where(lane // HEAD == head, spread[t * heads:(t + 1) * heads], F32(0.0)),
                axis=0, keepdims=True,
            )

    for piece in range(3):
        begin(piece, 0)
    out_local = pltpu.make_async_copy(wo_hbm, go.at[z], local.at[1])
    out_local.start()
    index_copy = pltpu.make_async_copy(index_hbm, index_ref, local.at[2])
    index_copy.start()
    out_copies = [
        remote(wo_hbm, go.at[z], send_o.at[i], recv_o.at[i], target)
        for i, target in enumerate(z_line)
    ]
    hidden_copy.wait()
    norm_rows()

    units = []
    waiting = []
    per_block = span // (2 * HEAD)
    for block in range(blocks):
        c = block * span
        units.append((2 * block, 2.5, functools.partial(project, gq, q_ref, c)))
        units += waiting[:2]
        waiting = waiting[2:]
        units.append((2 * block + 1, 2.5, functools.partial(project, gk, k_ref, c)))
        for pair in range(block * per_block, (block + 1) * per_block):
            for t in range(texts):
                waiting.append((2 * block + 1, 1.5, functools.partial(attend, pair, t)))
        units += waiting[:2]
        waiting = waiting[2:]
    units += waiting
    steps = len(pieces) + 3
    pace, clock, step = 4.2, 0.0, 0
    while units:
        if step < steps and (units[0][0] > step - 4 or clock >= pace * (step + 1)):
            advance(step)
            if step == 3:
                for copy in out_copies:
                    copy.start()
            step += 1
            clock = max(clock, pace * step)
        else:
            _, cost, run = units.pop(0)
            run()
            clock += cost
    stacked = combine()
    for block in range(blocks):
        while step < steps and step - 4 < 2 * blocks + block:
            advance(step)
            step += 1
        value_piece(stacked, block * span)

    def plane_device(step):
        return z * plane + lax.rem(place + step, plane)

    def plane_source(step):
        return lax.rem(place + plane - step, plane)

    def context_copy(step):
        return remote(
            context_mine, context_got.at[place], send_c.at[step], recv_c.at[step],
            plane_device(step),
        )

    for step in range(1, plane):
        context_copy(step).start()
    context_got[place] = context_mine[...]
    out_local.wait()
    for copy in out_copies:
        copy.wait()
    rows_out = go.shape[1]
    depth = planes * rows_out
    feature = lax.broadcasted_iota(jnp.int32, (features, depth), 0)
    slot = lax.broadcasted_iota(jnp.int32, (features, depth), 1)
    wanted = (slot // rows_out) * (plane * rows_out) + place * rows_out + lax.rem(slot, rows_out)
    choose = jnp.where(feature == wanted, 1.0, 0.0).astype(BF16)
    key_slot = lax.broadcasted_iota(jnp.int32, (16, lmax), 1)
    totals = []
    for t in range(texts):
        valid = jnp.where(key_slot < lengths_ref[t], 1.0, 0.0).astype(BF16)
        totals.append(
            jnp.dot(
                valid, hidden_ref[t * lmax:(t + 1) * lmax, :], preferred_element_type=F32
            )[0:1]
        )
    for step in range(1, plane):
        remote(
            context_mine, context_got.at[plane_source(step)], send_c.at[step],
            recv_c.at[step], plane_device(step),
        ).wait()
    for j in range(plane):
        context_flat[j * texts:(j + 1) * texts, :] = context_got[j]
    group = plane * texts
    chosen = jnp.dot(split_rows(context_flat[...]), choose, preferred_element_type=F32)
    held_out = go[...].reshape(depth, width).astype(BF16)
    part = jnp.dot(chosen.astype(BF16), held_out, preferred_element_type=F32)
    part = part[0:group] + part[group:2 * group]
    for j in range(plane):
        part_mine[j] = part[j * texts:(j + 1) * texts, :]

    def part_copy(step, where):
        return remote(
            part_mine.at[lax.rem(place + step, plane)], part_got.at[where], send_p.at[step],
            recv_p.at[step], plane_device(step),
        )

    for step in range(1, plane):
        part_copy(step, place).start()
    part_got[place] = part_mine[place]
    for step in range(1, plane):
        part_copy(step, plane_source(step)).wait()
    summed = part_got[0]
    for j in range(1, plane):
        summed += part_got[j]
    wide = width // 8
    for t in range(texts):
        pooled = (totals[t] + summed[t:t + 1]) / lengths_ref[t].astype(F32)
        mean = jnp.mean(pooled * pooled, axis=-1, keepdims=True)
        unit = pooled * lax.rsqrt(mean + 1e-06)
        for k in range(8):
            rows_ref[t * 8 + k:t * 8 + k + 1, 0:wide] = unit[:, k * wide:(k + 1) * wide]
        rows_ref[t * 8:(t + 1) * 8, wide:wide + 128] = jnp.full(
            (8, 128), order_ref[t], jnp.int32
        ).astype(F32)
    note_ref[...] = rows_ref[...].astype(BF16)

    line = [
        remote(note_ref, got.at[z, place], send_n.at[i], recv_n.at[i], target)
        for i, target in enumerate(z_line)
    ]
    for copy in line:
        copy.start()
    got[z, place] = note_ref[...]
    for copy in line:
        copy.wait()

    def note_copy(step, where):
        return remote(
            got.at[:, where], got.at[:, where], send_n.at[planes - 1 + step],
            recv_n.at[planes - 1 + step], plane_device(step),
        )

    for step in range(1, plane):
        note_copy(step, place).start()
    index_copy.wait()
    for step in range(1, plane):
        note_copy(step, place).wait_send()
        note_copy(step, plane_source(step)).wait_recv()

    total = count * texts
    rows_dev = index_ref.shape[0]
    long = count * texts * 8
    flat = got[...].reshape(long, wide + 128)
    data = flat[:, 0:wide]
    numbers = flat[:, wide:wide + 128].astype(F32).T[0:1, :].astype(jnp.int32)
    lane = lax.broadcasted_iota(jnp.int32, (total, long), 1)
    row = lax.broadcasted_iota(jnp.int32, (total, long), 0)
    same = numbers == row
    scores = jnp.zeros((total, rows_dev), F32)
    for k in range(8):
        pick = jnp.where(same & (lax.rem(lane, 8) == k), 1.0, 0.0).astype(BF16)
        unit = jnp.dot(pick, data, preferred_element_type=F32).astype(BF16)
        scores += lax.dot_general(
            unit, index_ref[:, k * wide:(k + 1) * wide], (((1,), (1,)), ((), ())),
            preferred_element_type=F32,
        )
    within = cand_ref[...] - me * rows_dev
    slot = lax.broadcasted_iota(jnp.int32, (1, 1, rows_dev), 2)
    for r in range(0, total, 8):
        hit = within[r:r + 8][:, :, None] == slot
        found = jnp.sum(jnp.where(hit, scores[r:r + 8][:, None, :], F32(0.0)), axis=2)
        for j in range(0, 8, texts):
            mine[(r + j) // texts] = found[j:j + texts, :]

    def back_copy(step, where):
        target = lax.rem(me + step, count)
        return remote(
            mine.at[target], back.at[where], send_s.at[step], recv_s.at[step], target
        )

    @pl.loop(1, count)
    def _(step):
        back_copy(step, me).start()

    back[me] = mine[me]

    @pl.loop(1, count)
    def _(step):
        back_copy(step, lax.rem(me + count - step, count)).wait()

    out_ref[...] = jnp.sum(back[...], axis=0)


def solution(mesh):
    count = mesh.shape["dp"]
    planes, rows, cols = grid_of(count)
    plane = rows * cols * 2

    def per_device(
        hidden, lengths, order, candidates, norm_gain, w_query, w_key, w_value, w_out, index_rows
    ):
        texts, lmax, width = hidden.shape
        slots, features = texts * lmax, w_query.shape[1]
        if w_out.shape[0] % 16:
            w_out = w_out.astype(F32)
        cand = candidates.shape[1]
        lead = (planes, rows, cols, 2)
        held = pltpu.VMEM(lead + w_query.shape, BF16)
        copies = planes - 1 + 2 * (rows - 1 + cols - 1) + 1
        pieces = 3 * features // 256
        note = (texts * 8, width // 8 + 128)
        dma = pltpu.SemaphoreType.DMA
        anywhere = pl.BlockSpec(memory_space=pl.ANY)
        scalar = pl.BlockSpec(memory_space=pltpu.SMEM)
        vector = pl.BlockSpec(memory_space=pltpu.VMEM)
        return pl.pallas_call(
            functools.partial(kernel, count),
            out_shape=jax.ShapeDtypeStruct((texts, cand), F32),
            in_specs=[scalar, scalar, anywhere, vector] + [anywhere] * 5 + [vector],
            out_specs=vector,
            scratch_shapes=[
                pltpu.VMEM((slots, width), BF16),
                pltpu.VMEM((slots, width), BF16),
                held, held, held,
                pltpu.VMEM((planes,) + w_out.shape, w_out.dtype),
                pltpu.VMEM((slots, features), BF16),
                pltpu.VMEM((slots, features), BF16),
                pltpu.VMEM((texts, features // HEAD // 2, 2 * lmax), F32),
                pltpu.VMEM(index_rows.shape, BF16),
                pltpu.VMEM((texts, features), F32),
                pltpu.VMEM((plane, texts, features), F32),
                pltpu.VMEM((plane * texts, features), F32),
                pltpu.VMEM((plane, texts, width), F32),
                pltpu.VMEM((plane, texts, width), F32),
                pltpu.VMEM(note, F32),
                pltpu.VMEM(note, BF16),
                pltpu.VMEM((planes, plane) + note, BF16),
                pltpu.VMEM((count, texts, cand), F32),
                pltpu.VMEM((count, texts, cand), F32),
                dma((pieces, copies)), dma((pieces, copies)), dma((pieces + 3,)),
                dma((planes,)), dma((planes,)), dma((plane,)), dma((plane,)),
                dma((plane,)), dma((plane,)), dma((planes + plane,)), dma((planes + plane,)),
                dma((count,)), dma((count,)),
            ],
            compiler_params=pltpu.CompilerParams(
                collective_id=0, has_side_effects=True, vmem_limit_bytes=56 * 1024 * 1024
            ),
            cost_estimate=pl.CostEstimate(
                flops=10 ** 10, bytes_accessed=24 * 2 ** 20, transcendentals=2 ** 23
            ),
        )(
            lengths, order, hidden.reshape(slots, width), norm_gain.reshape(1, width),
            w_query, w_key, w_value, w_out, index_rows, candidates,
        )

    return jax.shard_map(
        per_device,
        mesh=mesh,
        in_specs=(
            P("dp", None, None),
            P("dp"),
            P("dp"),
            P(),
            P(),
            P("dp", None),
            P("dp", None),
            P("dp", None),
            P("dp", None),
            P("dp", None),
        ),
        out_specs=P("dp", None),
        check_vma=False,
    )
```
